32 devices in a mesh: dp: 4 (over z), fsdp: 8 (over y, x, core).
Axes of the slice: x: 2, y: 2, z: 4, core: 2. Of those that a mesh axis runs over, the one named last changes fastest.
Arguments:
- hidden: bfloat16 [24576, 8192], P(('dp', 'fsdp')), may hold values from -6 to 6
- head: bfloat16 [512, 8192], P('fsdp'), may hold values from -0.0625 to 0.0625
- labels: int32 [24576], P(('dp', 'fsdp')), may hold values from 0 to 511
- lse: float32 [24576], P(('dp', 'fsdp')), may hold values from 0 to 1.5
- cotangent: float32 [24576], P(('dp', 'fsdp')), may hold values from -0.6 to 0.6
- block_lists: int32 [192, 4], P(('dp', 'fsdp')), may hold values from -1 to 3, as said below
Outputs:
- grad_hidden: bfloat16 [24576, 8192], P(('dp', 'fsdp'))
- grad_head: bfloat16 [512, 8192], P('fsdp', 'dp')
The draws below stay inside these ranges and needn't reach their ends.
Inputs may be any that keep to these rules, and one draw needn't show every extreme that they name: `block_lists`: each row names distinct vocabulary blocks in its first slots (at least one) and -1 in the remaining slots.
All inputs are finite; a program needn't handle non-finite values.
Results may differ from the reference program's by a relative error of at most 0.0056.
Values may be sent and summed in bfloat16 or wider, within the bound.
A program may use at most 192 MiB of HBM per device.

```python
import jax
import jax.numpy as jnp
from jax import lax

D = 8192
VB = 128
TB = 128
VBLOCKS = 4
T_DEV = 768
VOCAB = 512
TOKENS = 24576
NTB = 192


def draw_block_lists(key, part):
    blocks_all = TOKENS // TB
    groups = TOKENS // T_DEV
    per_group = T_DEV // TB
    key_level = jax.random.fold_in(key, 11)
    key_jitter = jax.random.fold_in(key, 23)
    key_order = jax.random.fold_in(key, 37)
    level = jax.random.randint(key_level, (groups,), 1, VBLOCKS + 1)
    level = jnp.repeat(level, per_group)
    jitter = jax.random.randint(key_jitter, (blocks_all,), -1, 2)
    count = jnp.clip(level + jitter, 1, VBLOCKS)
    scores = jax.random.randint(key_order, (blocks_all, VBLOCKS), 0, 1 << 20) * VBLOCKS + jnp.arange(VBLOCKS, dtype=jnp.int32)[None, :]
    order = jnp.argsort(scores, axis=1).astype(jnp.int32)
    slots = jnp.arange(VBLOCKS, dtype=jnp.int32)[None, :]
    return jnp.where(slots < count[:, None], order, -1).astype(jnp.int32)


def set_ends(values, rng, low, largest):
    dims = values.shape
    spot = [jax.random.randint(jax.random.fold_in(rng, axis), (), 0, dims[axis]) for axis in range(len(dims))]
    values = values.at[tuple(spot)].set(low)
    longest = dims.index(max(dims))
    spot[longest] = (spot[longest] + 1) % dims[longest]
    return values.at[tuple(spot)].set(largest)


def strengthened(array, key, source, target, shards_of, factor):
    owner, partner = [(jnp.arange(array.shape[dim]) // (array.shape[dim] // shards_of)).reshape([-1 if axis == dim else 1 for axis in range(array.ndim)]) for dim in (source, target)]
    chosen = jax.random.permutation(key, shards_of)[partner]
    strong = (owner == chosen) | (owner == (partner + shards_of // 2) % shards_of)
    return jnp.where(strong, factor * array, array)


def steps_of(own_key, shape, shards, low, high):
    gain, own = 1.0, jax.random.fold_in(own_key, 6)
    for position, shards_of in shards:
        draws = jnp.exp(jax.random.uniform(jax.random.fold_in(own, position), (shards_of,), jnp.float32, low / len(shards), high / len(shards)))
        gain = gain * jnp.repeat(draws, shape[position] // shards_of).reshape([-1 if axis == position else 1 for axis in range(len(shape))])
    return gain


def centred(stream_key, extent, width, reach, split=(), kind=jnp.bfloat16):
    entries = jax.random.normal(stream_key, extent, jnp.float32) * width
    if len(split) > 0:
        entries = steps_of(stream_key, extent, split, -0.22, 0.18) * entries
    return jnp.clip(entries, min=-reach, max=reach).astype(kind)


def bell_draw_with(key, extent, deviation, reach, pieces, heavy, held_as=jnp.bfloat16):
    result = deviation * jax.random.normal(key, extent, jnp.float32)
    if pieces:
        result = result * steps_of(key, extent, pieces, -0.22, 0.18)
    return jnp.clip(strengthened(result, jax.random.fold_in(key, 3), *heavy), -reach, reach).astype(held_as)


def setup_inputs(seed: int = 0) -> dict:
    seeds = jax.random.split(jax.random.key(seed), 7)
    hidden = bell_draw_with(seeds[0], (TOKENS, D), 1.0, 6.0, ((0, 32),), (0, 1, 32, 2.75))
    head = centred(seeds[1], (VOCAB, D), D ** -0.5, 0.0625, ((0, 8),))
    labels = set_ends(jax.random.randint(seeds[2], (TOKENS,), 0, VOCAB), jax.random.fold_in(seeds[2], 1), 0, VOCAB - 1).astype(jnp.int32)
    lse = jnp.clip(1.5 * jax.random.uniform(seeds[3], (TOKENS,), jnp.float32) ** steps_of(seeds[3], (TOKENS,), ((0, 32),), -0.2, 0.2), 0.0, 1.5)
    cotangent = centred(seeds[4], (TOKENS,), 0.1, 0.6, ((0, 32),), jnp.float32)
    block_lists = draw_block_lists(jax.random.fold_in(seeds[6], 71), 0)
    return {"hidden": hidden, "head": head, "labels": labels, "lse": lse, "cotangent": cotangent, "block_lists": block_lists}


def reference(hidden, head, labels, lse, cotangent, block_lists):
    listed = jnp.any(block_lists[:, :, None] == jnp.arange(VBLOCKS, dtype=jnp.int32)[None, None, :], axis=1)
    mask = jnp.repeat(listed, VB, axis=1).astype(jnp.float32)
    columns = jnp.arange(VB * VBLOCKS, dtype=jnp.int32)
    hidden_blocks = hidden.reshape(NTB, TB, D)
    label_blocks = labels.reshape(NTB, TB)
    lse_blocks = lse.reshape(NTB, TB)
    cot_blocks = cotangent.reshape(NTB, TB)

    def advance(total, items):
        rows, targets, norms, scales, keep = items
        logits = jnp.dot(rows, head.T, preferred_element_type=jnp.float32)
        hits = (targets[:, None] == columns[None, :]).astype(jnp.float32)
        grad_logits = (scales[:, None] * (keep[None, :] * jnp.exp(logits - norms[:, None]) - hits)).astype(jnp.bfloat16)
        grad_rows = jnp.dot(grad_logits, head, preferred_element_type=jnp.float32).astype(jnp.bfloat16)
        total = total + jnp.dot(grad_logits.T, rows, preferred_element_type=jnp.float32)
        return total, grad_rows

    start = jnp.zeros((VB * VBLOCKS, D), jnp.float32)
    total, grad_rows = lax.scan(advance, start, (hidden_blocks, label_blocks, lse_blocks, cot_blocks, mask))
    return grad_rows.reshape(NTB * TB, D), total.astype(jnp.bfloat16)
```

```python
import jax
import jax.numpy as jnp
from jax import lax
from jax.experimental import pallas as pl
from jax.experimental.pallas import tpu as pltpu
from jax.sharding import PartitionSpec as P

VB = 128
VBLOCKS = 4
MESH = pl.DeviceIdType.MESH
F32 = jnp.float32
BF16 = jnp.bfloat16


def listed_of(block_lists):
    ids = jnp.arange(VBLOCKS, dtype=jnp.int32)
    return jnp.any(block_lists[:, :, None] == ids[None, None, :], axis=1)


def plain(hidden, head, labels, lse, cotangent, block_lists):
    tokens = hidden.shape[0]
    full_head = lax.all_gather(head, "fsdp", axis=0, tiled=True)
    vocab = full_head.shape[0]
    keep = jnp.repeat(listed_of(block_lists), tokens // block_lists.shape[0], axis=0)
    keep = jnp.repeat(keep, VB, axis=1)
    logits = lax.dot_general(hidden, full_head, (((1,), (1,)), ((), ())), preferred_element_type=F32)
    hits = (labels[:, None] == jnp.arange(vocab, dtype=jnp.int32)[None, :]).astype(F32)
    soft = jnp.where(keep, jnp.exp(logits - lse[:, None]), 0.0)
    grad_logits = (cotangent[:, None] * (soft - hits)).astype(BF16)
    grad_hidden = jnp.dot(grad_logits, full_head, preferred_element_type=F32).astype(BF16)
    term = lax.dot_general(grad_logits, hidden, (((0,), (0,)), ((), ())), preferred_element_type=F32)
    slab = lax.psum_scatter(term, "fsdp", scatter_dimension=0, tiled=True)
    owned = lax.psum_scatter(slab, "dp", scatter_dimension=1, tiled=True)
    return grad_hidden, owned.astype(BF16)


def kernel(
    hid_hbm, head_hbm, aux, gl_hbm, head_out, out,
    hid, headv, acc, gl, glt, own, tosib, fromsib, part, relay, got, zs, zgot,
    s_hid, s_own, s_out, ag_s, ag_r, sib_s, sib_r, rs_s, rs_r, z_s, z_r,
):
    tokens, width = hid.shape
    rows = head_hbm.shape[0]
    half = width // 2
    quarter = width // 4
    tile = 512
    dp = lax.axis_index("dp")
    f = lax.axis_index("fsdp")
    core, x, y = f % 2, (f // 2) % 2, f // 4
    sib = (dp, f + 1 - 2 * core)
    dev_x = (dp, f + 2 - 4 * x)
    dev_y = (dp, f + 4 - 8 * y)
    zdev = [((dp + r) % 4, f) for r in (1, 2, 3)]

    loads = [
        pltpu.make_async_copy(
            hid_hbm.at[:, pl.ds(i * quarter, quarter)], hid.at[:, pl.ds(i * quarter, quarter)], s_hid.at[i]
        )
        for i in range(4)
    ]
    for c in loads:
        c.start()
    own_copy = pltpu.make_async_copy(head_hbm, headv.at[0], s_own)
    own_copy.start()

    barrier = pltpu.get_barrier_semaphore()
    for d in [sib, dev_x, dev_y] + zdev:
        pl.semaphore_signal(barrier, inc=1, device_id=d, device_id_type=MESH)
    pl.semaphore_wait(barrier, 6)

    sent = []

    def send(src, dst, ssem, rsem, dev):
        c = pltpu.make_async_remote_copy(
            src_ref=src, dst_ref=dst, send_sem=ssem, recv_sem=rsem, device_id=dev, device_id_type=MESH
        )
        c.start()
        sent.append(c)
        return c

    def ag(src, dst, i, dev):
        return send(src, dst, ag_s.at[i], ag_r.at[i], dev)

    lo, hi = pl.ds(0, half), pl.ds(half, half)
    a_x = ag(head_hbm, headv.at[2], 0, dev_x)
    a_y = ag(head_hbm, headv.at[4], 1, dev_y)
    a_sib = ag(head_hbm, headv.at[1], 2, sib)

    def gradients(j):
        acc[...] = jnp.zeros_like(acc)

        @pl.loop(0, width // 1024)
        def _(i):
            cols = pl.ds(pl.multiple_of(i * 1024, 1024), 1024)
            rows_j = headv[2 * j : 2 * j + 2, :, cols].reshape(2 * rows, 1024)
            acc[...] += lax.dot_general(
                hid[:, cols], rows_j, (((1,), (1,)), ((), ())), preferred_element_type=F32
            )

        lse, cot, spot, keep = aux[:, 0:1], aux[:, 1:2], aux[:, 2:3], aux[:, 4 + j : 5 + j]
        ids = lax.broadcasted_iota(jnp.int32, acc.shape, 1) + 2 * rows * j
        hits = jnp.where(ids.astype(F32) == spot, 1.0, 0.0)
        g = cot * (jnp.where(keep > 0.5, jnp.exp(acc[...] - lse), 0.0) - hits)
        gl[:, 2 * rows * j : 2 * rows * (j + 1)] = g.astype(BF16)
        glt[j] = g.T.astype(BF16)

        @pl.loop(0, width // tile)
        def _(i):
            cols = pl.ds(pl.multiple_of(i * tile, tile), tile)
            t = jnp.dot(glt[j], hid[:, cols], preferred_element_type=F32)
            own[j, :, cols] = t[:rows]
            tosib[j, :, cols] = t[rows:].astype(BF16)

        return send(tosib.at[j], fromsib.at[j], sib_s.at[j], sib_r.at[j], sib)

    def pair_sum(j, c):
        c.wait_recv()

        @pl.loop(0, width // tile)
        def _(i):
            cols = pl.ds(pl.multiple_of(i * tile, tile), tile)
            total = own[j, :, cols] + fromsib[j, :, cols].astype(F32)
            if j == 0:
                own[0, :, cols] = total
            else:
                part[j - 1, :, cols] = total.astype(BF16)

    for c in loads:
        c.wait()
    own_copy.wait()
    a_sib.wait_recv()
    c0 = gradients(0)
    a_x.wait_recv()
    r_y = ag(headv.at[2, :, lo], headv.at[6, :, lo], 3, dev_y)
    f_x = ag(headv.at[2], headv.at[3], 4, sib)
    a_y.wait_recv()
    r_x = ag(headv.at[4, :, hi], headv.at[6, :, hi], 5, dev_x)
    f_y = ag(headv.at[4], headv.at[5], 6, sib)
    pair_sum(0, c0)
    f_x.wait_recv()
    c1 = gradients(1)
    pair_sum(1, c1)
    d_x = send(part.at[0, :, lo], got.at[0, :, lo], rs_s.at[0], rs_r.at[0], dev_x)
    r_y.wait_recv()
    f_lo = ag(headv.at[6, :, lo], headv.at[7, :, lo], 7, sib)
    r_x.wait_recv()
    f_hi = ag(headv.at[6, :, hi], headv.at[7, :, hi], 8, sib)
    f_y.wait_recv()
    c2 = gradients(2)
    pair_sum(2, c2)
    d_y = send(part.at[1, :, hi], got.at[1, :, hi], rs_s.at[1], rs_r.at[1], dev_y)
    f_lo.wait_recv()
    f_hi.wait_recv()
    c3 = gradients(3)
    keep_head = pltpu.make_async_copy(headv, head_out, s_out.at[0])
    keep_head.start()
    keep_gl = pltpu.make_async_copy(gl, gl_hbm, s_out.at[1])
    keep_gl.start()
    pair_sum(3, c3)
    v_x = send(part.at[2, :, lo], relay.at[:, lo], rs_s.at[2], rs_r.at[2], dev_x)
    v_y = send(part.at[2, :, hi], relay.at[:, hi], rs_s.at[3], rs_r.at[3], dev_y)

    def joined(c, p, first):
        c.wait_recv()

        @pl.loop(0, half // tile)
        def _(i):
            cols = pl.ds(pl.multiple_of(first + i * tile, tile), tile)
            part[p, :, cols] = (part[p, :, cols].astype(F32) + relay[:, cols].astype(F32)).astype(BF16)

    joined(v_x, 1, 0)
    e_y = send(part.at[1, :, lo], got.at[1, :, lo], rs_s.at[4], rs_r.at[4], dev_y)
    joined(v_y, 0, half)
    e_x = send(part.at[0, :, hi], got.at[0, :, hi], rs_s.at[5], rs_r.at[5], dev_x)
    for c in (d_x, d_y, e_y, e_x):
        c.wait_recv()

    def slab_sum(first, i):
        cols = pl.ds(pl.multiple_of(first + i * tile, tile), tile)
        return own[0, :, cols] + got[0, :, cols].astype(F32) + got[1, :, cols].astype(F32)

    zc = []
    for r in (2, 1, 3):

        @pl.loop(0, quarter // tile)
        def _(i):
            zs[r - 1, :, pl.ds(pl.multiple_of(i * tile, tile), tile)] = slab_sum(
                ((dp + r) % 4) * quarter, i
            ).astype(BF16)

        zc.append(send(zs.at[r - 1], zgot.at[r - 1], z_s.at[r - 1], z_r.at[r - 1], zdev[r - 1]))
    for c in zc:
        c.wait_recv()

    @pl.loop(0, quarter // tile)
    def _(i):
        cols = pl.ds(pl.multiple_of(i * tile, tile), tile)
        total = slab_sum(dp * quarter, i)
        for r in range(3):
            total = total + zgot[r, :, cols].astype(F32)
        out[:, cols] = total.astype(BF16)

    for c in sent:
        c.wait_send()
    keep_head.wait()
    keep_gl.wait()


def fused(hidden, head, labels, lse, cotangent, block_lists):
    tokens, width = hidden.shape
    rows = head.shape[0]
    f = lax.axis_index("fsdp")
    listed = listed_of(block_lists).astype(F32)
    order = jnp.arange(VBLOCKS, dtype=jnp.int32) ^ (f // 2)
    mine = jnp.sum(
        jnp.where(order[None, :, None] == jnp.arange(VBLOCKS)[None, None, :], listed[:, None, :], 0.0), axis=2
    )
    keep = jnp.repeat(mine, tokens // block_lists.shape[0], axis=0)
    spot = ((labels // rows) ^ f) * rows + labels % rows
    aux = jnp.concatenate(
        [lse[:, None], cotangent[:, None], spot.astype(F32)[:, None], jnp.zeros((tokens, 1), F32), keep,
         jnp.zeros((tokens, 120), F32)], axis=1,
    )
    vm = pltpu.VMEM
    dma = pltpu.SemaphoreType.DMA
    any_ = pl.BlockSpec(memory_space=pl.ANY)
    vmem = pl.BlockSpec(memory_space=pltpu.VMEM)
    gl, full, owned = pl.pallas_call(
        kernel,
        out_shape=(
            jax.ShapeDtypeStruct((tokens, 8 * rows), BF16),
            jax.ShapeDtypeStruct((8, rows, width), BF16),
            jax.ShapeDtypeStruct((rows, width // 4), BF16),
        ),
        in_specs=[any_, any_, vmem],
        out_specs=(any_, any_, vmem),
        scratch_shapes=[
            vm((tokens, width), BF16), vm((8, rows, width), BF16), vm((tokens, 2 * rows), F32),
            vm((tokens, 8 * rows), BF16), vm((4, 2 * rows, tokens), BF16),
            vm((4, rows, width), F32), vm((4, rows, width), BF16), vm((4, rows, width), BF16),
            vm((3, rows, width), BF16), vm((rows, width), BF16), vm((2, rows, width), BF16),
            vm((3, rows, width // 4), BF16), vm((3, rows, width // 4), BF16),
            dma((4,)), dma, dma((2,)), dma((9,)), dma((9,)), dma((4,)), dma((4,)),
            dma((6,)), dma((6,)), dma((3,)), dma((3,)),
        ],
        compiler_params=pltpu.CompilerParams(
            collective_id=0, has_side_effects=True, vmem_limit_bytes=58 * 1024 * 1024
        ),
    )(hidden, head, aux)
    grad_hidden = jnp.dot(gl, full.reshape(8 * rows, width), preferred_element_type=F32).astype(BF16)
    return grad_hidden, owned


def solution(mesh):
    small = mesh.shape["dp"] == 4 and mesh.shape["fsdp"] == 8
    return jax.shard_map(
        fused if small else plain,
        mesh=mesh,
        in_specs=(
            P(("dp", "fsdp"), None),
            P("fsdp", None),
            P(("dp", "fsdp")),
            P(("dp", "fsdp")),
            P(("dp", "fsdp")),
            P(("dp", "fsdp"), None),
        ),
        out_specs=(P(("dp", "fsdp"), None), P("fsdp", "dp")),
        check_vma=False,
    )
```

```python
import jax
import jax.numpy as jnp
from jax import lax
from jax.experimental import pallas as pl
from jax.experimental.pallas import tpu as pltpu
from jax.sharding import PartitionSpec as P

VB = 128
VBLOCKS = 4
MESH = pl.DeviceIdType.MESH
F32 = jnp.float32
BF16 = jnp.bfloat16


def listed_of(block_lists):
    ids = jnp.arange(VBLOCKS, dtype=jnp.int32)
    return jnp.any(block_lists[:, :, None] == ids[None, None, :], axis=1)


def plain(hidden, head, labels, lse, cotangent, block_lists):
    tokens = hidden.shape[0]
    full_head = lax.all_gather(head, "fsdp", axis=0, tiled=True)
    vocab = full_head.shape[0]
    keep = jnp.repeat(listed_of(block_lists), tokens // block_lists.shape[0], axis=0)
    keep = jnp.repeat(keep, VB, axis=1)
    logits = lax.dot_general(hidden, full_head, (((1,), (1,)), ((), ())), preferred_element_type=F32)
    hits = (labels[:, None] == jnp.arange(vocab, dtype=jnp.int32)[None, :]).astype(F32)
    soft = jnp.where(keep, jnp.exp(logits - lse[:, None]), 0.0)
    grad_logits = (cotangent[:, None] * (soft - hits)).astype(BF16)
    grad_hidden = jnp.dot(grad_logits, full_head, preferred_element_type=F32).astype(BF16)
    term = lax.dot_general(grad_logits, hidden, (((0,), (0,)), ((), ())), preferred_element_type=F32)
    slab = lax.psum_scatter(term, "fsdp", scatter_dimension=0, tiled=True)
    owned = lax.psum_scatter(slab, "dp", scatter_dimension=1, tiled=True)
    return grad_hidden, owned.astype(BF16)


def kernel(
    hid_hbm, head_hbm, aux, gl_hbm, head_out, out,
    hid, headv, acc, gl, glt, own, tosib, fromsib, part, relay, got, zs, zgot,
    s_hid, s_own, s_out, ag_s, ag_r, sib_s, sib_r, rs_s, rs_r, z_s, z_r,
):
    tokens, width = hid.shape
    rows = head_hbm.shape[0]
    half = width // 2
    quarter = width // 4
    tile = 512
    dp = lax.axis_index("dp")
    f = lax.axis_index("fsdp")
    core, x, y = f % 2, (f // 2) % 2, f // 4
    sib = (dp, f + 1 - 2 * core)
    dev_x = (dp, f + 2 - 4 * x)
    dev_y = (dp, f + 4 - 8 * y)
    zdev = [((dp + r) % 4, f) for r in (1, 2, 3)]

    loads = [
        pltpu.make_async_copy(
            hid_hbm.at[:, pl.ds(i * quarter, quarter)], hid.at[:, pl.ds(i * quarter, quarter)], s_hid.at[i]
        )
        for i in range(4)
    ]
    for c in loads:
        c.start()
    own_copy = pltpu.make_async_copy(head_hbm, headv.at[0], s_own)
    own_copy.start()

    barrier = pltpu.get_barrier_semaphore()
    for d in [sib, dev_x, dev_y] + zdev:
        pl.semaphore_signal(barrier, inc=1, device_id=d, device_id_type=MESH)
    pl.semaphore_wait(barrier, 6)

    sent = []

    def send(src, dst, ssem, rsem, dev):
        c = pltpu.make_async_remote_copy(
            src_ref=src, dst_ref=dst, send_sem=ssem, recv_sem=rsem, device_id=dev, device_id_type=MESH
        )
        c.start()
        sent.append(c)
        return c

    def ag(src, dst, i, dev):
        return send(src, dst, ag_s.at[i], ag_r.at[i], dev)

    lo, hi = pl.ds(0, half), pl.ds(half, half)
    a_x = ag(head_hbm, headv.at[2], 0, dev_x)
    a_y = ag(head_hbm, headv.at[4], 1, dev_y)
    a_sib = ag(head_hbm, headv.at[1], 2, sib)

    def cols_at(first, i):
        return pl.ds(pl.multiple_of(first + i * tile, tile), tile)

    def piece(p):
        return pl.ds(p * quarter, quarter)

    def logits_grad(j):
        acc[...] = jnp.zeros_like(acc)

        @pl.loop(0, width // 1024)
        def _(i):
            cols = pl.ds(pl.multiple_of(i * 1024, 1024), 1024)
            rows_j = headv[2 * j : 2 * j + 2, :, cols].reshape(2 * rows, 1024)
            acc[...] += lax.dot_general(
                rows_j, hid[:, cols], (((1,), (1,)), ((), ())), preferred_element_type=F32
            )

        lse, cot, spot, keep = aux[0:1, :], aux[1:2, :], aux[2:3, :], aux[4 + j : 5 + j, :]
        ids = lax.broadcasted_iota(jnp.int32, acc.shape, 0) + 2 * rows * j
        hits = jnp.where(ids.astype(F32) == spot, 1.0, 0.0)
        g = cot * (jnp.where(keep > 0.5, jnp.exp(acc[...] - lse), 0.0) - hits)
        glt[j] = g.astype(BF16)
        gl[:, 2 * rows * j : 2 * rows * (j + 1)] = g.T.astype(BF16)

    def terms(j, p):
        @pl.loop(0, quarter // tile)
        def _(i):
            t = jnp.dot(glt[j], hid[:, cols_at(p * tile, i * 4)], preferred_element_type=F32)
            cols = cols_at(p * quarter, i)
            own[j, :, cols] = t[:rows]
            tosib[j, :, cols] = t[rows:].astype(BF16)

    def gradients(j):
        logits_grad(j)
        for p in range(4):
            terms(j, p)
        return send(tosib.at[j], fromsib.at[j], sib_s.at[j], sib_r.at[j], sib)

    def add_pair(j, first, count):
        @pl.loop(0, count)
        def _(i):
            cols = cols_at(first, i)
            total = own[j, :, cols] + fromsib[j, :, cols].astype(F32)
            if j == 0:
                own[0, :, cols] = total
            else:
                part[j - 1, :, cols] = total.astype(BF16)

    def pair_sum(j, c):
        c.wait_recv()
        add_pair(j, 0, width // tile)

    for c in loads:
        c.wait()
    own_copy.wait()
    a_sib.wait_recv()
    c0 = gradients(0)
    a_x.wait_recv()
    r_y = ag(headv.at[2, :, lo], headv.at[6, :, lo], 3, dev_y)
    f_x = ag(headv.at[2], headv.at[3], 4, sib)
    a_y.wait_recv()
    r_x = ag(headv.at[4, :, hi], headv.at[6, :, hi], 5, dev_x)
    f_y = ag(headv.at[4], headv.at[5], 6, sib)
    pair_sum(0, c0)
    f_x.wait_recv()
    c1 = gradients(1)
    pair_sum(1, c1)
    d_x = send(part.at[0, :, lo], got.at[0, :, lo], rs_s.at[0], rs_r.at[0], dev_x)
    r_y.wait_recv()
    f_lo = ag(headv.at[6, :, lo], headv.at[7, :, lo], 7, sib)
    r_x.wait_recv()
    f_hi = ag(headv.at[6, :, hi], headv.at[7, :, hi], 8, sib)
    f_y.wait_recv()
    c2 = gradients(2)
    pair_sum(2, c2)
    d_y = send(part.at[1, :, hi], got.at[1, :, hi], rs_s.at[1], rs_r.at[1], dev_y)
    f_lo.wait_recv()
    f_hi.wait_recv()
    logits_grad(3)
    keep_head = pltpu.make_async_copy(headv, head_out, s_out.at[0])
    keep_head.start()
    keep_gl = pltpu.make_async_copy(gl, gl_hbm, s_out.at[1])
    keep_gl.start()
    order = (0, 2, 1, 3)
    cs, vs, es = {}, {}, {}

    def pass_on(p):
        cs[p].wait_recv()
        add_pair(3, p * quarter, quarter // tile)
        vs[p] = send(
            part.at[2, :, piece(p)], relay.at[:, piece(p)], rs_s.at[2 + p], rs_r.at[2 + p], dev_x if p < 2 else dev_y
        )

    for i in range(4):
        p = order[i]
        terms(3, p)
        cs[p] = send(
            tosib.at[3, :, piece(p)], fromsib.at[3, :, piece(p)], sib_s.at[3 + p], sib_r.at[3 + p], sib
        )
        if i > 0:
            pass_on(order[i - 1])
    pass_on(order[3])

    for p in order:
        vs[p].wait_recv()
        k = 1 if p < 2 else 0

        @pl.loop(0, quarter // tile)
        def _(i):
            cols = cols_at(p * quarter, i)
            part[k, :, cols] = (part[k, :, cols].astype(F32) + relay[:, cols].astype(F32)).astype(BF16)

        es[p] = send(
            part.at[k, :, piece(p)], got.at[k, :, piece(p)], rs_s.at[6 + p], rs_r.at[6 + p], dev_y if p < 2 else dev_x
        )

    def slab_sum(p, q):
        cols = cols_at(p * quarter, q)
        return own[0, :, cols] + got[0, :, cols].astype(F32) + got[1, :, cols].astype(F32)

    zc = {}
    for p in order:
        if p == order[0]:
            d_x.wait_recv()
        if p == order[1]:
            d_y.wait_recv()
        es[p].wait_recv()
        here = pl.ds(p * tile, tile)
        for r in (2, 1, 3):
            zs[r - 1, :, here] = slab_sum(p, (dp + r) % 4).astype(BF16)
            n = 3 * p + r - 1
            zc[p, r] = send(
                zs.at[r - 1, :, here], zgot.at[r - 1, :, here], z_s.at[n], z_r.at[n], zdev[r - 1]
            )
    for p in order:
        here = pl.ds(p * tile, tile)
        total = slab_sum(p, dp)
        for r in (1, 2, 3):
            zc[p, r].wait_recv()
            total = total + zgot[r - 1, :, here].astype(F32)
        out[:, here] = total.astype(BF16)

    for c in sent:
        c.wait_send()
    keep_head.wait()
    keep_gl.wait()


def rows_kernel(gl, head, out):
    out[...] = jnp.dot(gl[...], head[...], preferred_element_type=F32).astype(BF16)


def fused(hidden, head, labels, lse, cotangent, block_lists):
    tokens, width = hidden.shape
    rows = head.shape[0]
    f = lax.axis_index("fsdp")
    listed = listed_of(block_lists).astype(F32)
    order = jnp.arange(VBLOCKS, dtype=jnp.int32) ^ (f // 2)
    mine = jnp.sum(
        jnp.where(order[:, None, None] == jnp.arange(VBLOCKS)[None, None, :], listed[None, :, :], 0.0), axis=2
    )
    keep = jnp.repeat(mine, tokens // block_lists.shape[0], axis=1)
    spot = ((labels // rows) ^ f) * rows + labels % rows
    aux = jnp.concatenate(
        [lse[None], cotangent[None], spot.astype(F32)[None], jnp.zeros((1, tokens), F32), keep], axis=0
    )
    vm = pltpu.VMEM
    dma = pltpu.SemaphoreType.DMA
    any_ = pl.BlockSpec(memory_space=pl.ANY)
    vmem = pl.BlockSpec(memory_space=pltpu.VMEM)
    gl, full, owned = pl.pallas_call(
        kernel,
        out_shape=(
            jax.ShapeDtypeStruct((tokens, 8 * rows), BF16),
            jax.ShapeDtypeStruct((8, rows, width), BF16),
            jax.ShapeDtypeStruct((rows, width // 4), BF16),
        ),
        in_specs=[any_, any_, vmem],
        out_specs=(any_, any_, vmem),
        scratch_shapes=[
            vm((tokens, width), BF16), vm((8, rows, width), BF16), vm((2 * rows, tokens), F32),
            vm((tokens, 8 * rows), BF16), vm((4, 2 * rows, tokens), BF16),
            vm((4, rows, width), F32), vm((4, rows, width), BF16), vm((4, rows, width), BF16),
            vm((3, rows, width), BF16), vm((rows, width), BF16), vm((2, rows, width), BF16),
            vm((3, rows, width // 4), BF16), vm((3, rows, width // 4), BF16),
            dma((4,)), dma, dma((2,)), dma((9,)), dma((9,)), dma((7,)), dma((7,)),
            dma((10,)), dma((10,)), dma((12,)), dma((12,)),
        ],
        compiler_params=pltpu.CompilerParams(
            collective_id=0, has_side_effects=True, vmem_limit_bytes=58 * 1024 * 1024
        ),
    )(hidden, head, aux)
    wide = 1024
    grad_hidden = pl.pallas_call(
        rows_kernel,
        out_shape=jax.ShapeDtypeStruct((tokens, width), BF16),
        grid=(width // wide,),
        in_specs=[
            pl.BlockSpec((tokens, 8 * rows), lambda i: (0, 0)),
            pl.BlockSpec((8 * rows, wide), lambda i: (0, i)),
        ],
        out_specs=pl.BlockSpec((tokens, wide), lambda i: (0, i)),
        compiler_params=pltpu.CompilerParams(vmem_limit_bytes=60 * 1024 * 1024),
    )(gl, full.reshape(8 * rows, width))
    return grad_hidden, owned


def solution(mesh):
    small = mesh.shape["dp"] == 4 and mesh.shape["fsdp"] == 8
    return jax.shard_map(
        fused if small else plain,
        mesh=mesh,
        in_specs=(
            P(("dp", "fsdp"), None),
            P("fsdp", None),
            P(("dp", "fsdp")),
            P(("dp", "fsdp")),
            P(("dp", "fsdp")),
            P(("dp", "fsdp"), None),
        ),
        out_specs=(P(("dp", "fsdp"), None), P("fsdp", "dp")),
        check_vma=False,
    )
```

```python
import jax
import jax.numpy as jnp
from jax import lax
from jax.experimental import pallas as pl
from jax.experimental.pallas import tpu as pltpu
from jax.sharding import PartitionSpec as P

VB = 128
VBLOCKS = 4
MESH = pl.DeviceIdType.MESH
F32 = jnp.float32
BF16 = jnp.bfloat16


def listed_of(block_lists):
    ids = jnp.arange(VBLOCKS, dtype=jnp.int32)
    return jnp.any(block_lists[:, :, None] == ids[None, None, :], axis=1)


def plain(hidden, head, labels, lse, cotangent, block_lists):
    tokens = hidden.shape[0]
    full_head = lax.all_gather(head, "fsdp", axis=0, tiled=True)
    vocab = full_head.shape[0]
    keep = jnp.repeat(listed_of(block_lists), tokens // block_lists.shape[0], axis=0)
    keep = jnp.repeat(keep, VB, axis=1)
    logits = lax.dot_general(hidden, full_head, (((1,), (1,)), ((), ())), preferred_element_type=F32)
    hits = (labels[:, None] == jnp.arange(vocab, dtype=jnp.int32)[None, :]).astype(F32)
    soft = jnp.where(keep, jnp.exp(logits - lse[:, None]), 0.0)
    grad_logits = (cotangent[:, None] * (soft - hits)).astype(BF16)
    grad_hidden = jnp.dot(grad_logits, full_head, preferred_element_type=F32).astype(BF16)
    term = lax.dot_general(grad_logits, hidden, (((0,), (0,)), ((), ())), preferred_element_type=F32)
    slab = lax.psum_scatter(term, "fsdp", scatter_dimension=0, tiled=True)
    owned = lax.psum_scatter(slab, "dp", scatter_dimension=1, tiled=True)
    return grad_hidden, owned.astype(BF16)


def kernel(
    hid_hbm, head_hbm, aux, gl_hbm, head_out, out,
    hid, headv, acc, gl, glt, own, tosib, fromsib, part, relay, got, zs, zgot,
    s_hid, s_own, s_out, ag_s, ag_r, sib_s, sib_r, rs_s, rs_r, z_s, z_r,
):
    tokens, width = hid.shape
    rows = head_hbm.shape[0]
    half = width // 2
    quarter = width // 4
    tile = 512
    dp = lax.axis_index("dp")
    f = lax.axis_index("fsdp")
    core, x, y = f % 2, (f // 2) % 2, f // 4
    sib = (dp, f + 1 - 2 * core)
    dev_x = (dp, f + 2 - 4 * x)
    dev_y = (dp, f + 4 - 8 * y)
    zdev = [((dp + r) % 4, f) for r in (1, 2, 3)]

    loads = [
        pltpu.make_async_copy(
            hid_hbm.at[:, pl.ds(i * quarter, quarter)], hid.at[:, pl.ds(i * quarter, quarter)], s_hid.at[i]
        )
        for i in range(4)
    ]
    for c in loads:
        c.start()
    own_copy = pltpu.make_async_copy(head_hbm, headv.at[0], s_own)
    own_copy.start()

    barrier = pltpu.get_barrier_semaphore()
    for d in [sib, dev_x, dev_y] + zdev:
        pl.semaphore_signal(barrier, inc=1, device_id=d, device_id_type=MESH)
    pl.semaphore_wait(barrier, 6)

    sent = []

    def send(src, dst, ssem, rsem, dev):
        c = pltpu.make_async_remote_copy(
            src_ref=src, dst_ref=dst, send_sem=ssem, recv_sem=rsem, device_id=dev, device_id_type=MESH
        )
        c.start()
        sent.append(c)
        return c

    def ag(src, dst, i, dev):
        return send(src, dst, ag_s.at[i], ag_r.at[i], dev)

    lo, hi = pl.ds(0, half), pl.ds(half, half)
    a_x = ag(head_hbm, headv.at[2], 0, dev_x)
    a_y = ag(head_hbm, headv.at[4], 1, dev_y)
    a_sib = ag(head_hbm, headv.at[1], 2, sib)

    def cols_at(first, i):
        return pl.ds(pl.multiple_of(first + i * tile, tile), tile)

    def piece(p):
        return pl.ds(p * quarter, quarter)

    def logits_grad(j):
        acc[...] = jnp.zeros_like(acc)

        @pl.loop(0, width // 1024)
        def _(i):
            cols = pl.ds(pl.multiple_of(i * 1024, 1024), 1024)
            rows_j = headv[2 * j : 2 * j + 2, :, cols].reshape(2 * rows, 1024)
            acc[...] += lax.dot_general(
                rows_j, hid[:, cols], (((1,), (1,)), ((), ())), preferred_element_type=F32
            )

        lse, cot, spot, keep = aux[0:1, :], aux[1:2, :], aux[2:3, :], aux[4 + j : 5 + j, :]
        ids = lax.broadcasted_iota(jnp.int32, acc.shape, 0) + 2 * rows * j
        hits = jnp.where(ids.astype(F32) == spot, 1.0, 0.0)
        g = cot * (jnp.where(keep > 0.5, jnp.exp(acc[...] - lse), 0.0) - hits)
        glt[j] = g.astype(BF16)
        gl[:, 2 * rows * j : 2 * rows * (j + 1)] = g.T.astype(BF16)

    def terms(j, p):
        @pl.loop(0, quarter // tile)
        def _(i):
            t = jnp.dot(glt[j], hid[:, cols_at(p * tile, i * 4)], preferred_element_type=F32)
            cols = cols_at(p * quarter, i)
            own[j, :, cols] = t[:rows]
            tosib[j, :, cols] = t[rows:].astype(BF16)

    def gradients(j):
        logits_grad(j)
        for p in range(4):
            terms(j, p)
        return send(tosib.at[j], fromsib.at[j], sib_s.at[j], sib_r.at[j], sib)

    def add_pair(j, first, count):
        @pl.loop(0, count)
        def _(i):
            cols = cols_at(first, i)
            total = own[j, :, cols] + fromsib[j, :, cols].astype(F32)
            if j == 0:
                own[0, :, cols] = total
            else:
                part[j - 1, :, cols] = total.astype(BF16)

    def pair_sum(j, c):
        c.wait_recv()
        add_pair(j, 0, width // tile)

    for c in loads:
        c.wait()
    own_copy.wait()
    a_sib.wait_recv()
    c0 = gradients(0)
    a_x.wait_recv()
    r_y = ag(headv.at[2, :, lo], headv.at[6, :, lo], 3, dev_y)
    f_x = ag(headv.at[2], headv.at[3], 4, sib)
    a_y.wait_recv()
    r_x = ag(headv.at[4, :, hi], headv.at[6, :, hi], 5, dev_x)
    f_y = ag(headv.at[4], headv.at[5], 6, sib)
    pair_sum(0, c0)
    f_x.wait_recv()
    c1 = gradients(1)
    pair_sum(1, c1)
    d_x = send(part.at[0, :, lo], got.at[0, :, lo], rs_s.at[0], rs_r.at[0], dev_x)
    f_y.wait_recv()
    c2 = gradients(2)
    r_y.wait_recv()
    f_lo = ag(headv.at[6, :, lo], headv.at[7, :, lo], 7, sib)
    r_x.wait_recv()
    f_hi = ag(headv.at[6, :, hi], headv.at[7, :, hi], 8, sib)
    pair_sum(2, c2)
    d_y = send(part.at[1, :, hi], got.at[1, :, hi], rs_s.at[1], rs_r.at[1], dev_y)
    f_lo.wait_recv()
    f_hi.wait_recv()
    logits_grad(3)
    keep_head = pltpu.make_async_copy(headv, head_out, s_out.at[0])
    keep_head.start()
    keep_gl = pltpu.make_async_copy(gl, gl_hbm, s_out.at[1])
    keep_gl.start()
    order = (0, 2, 1, 3)
    cs, vs, es = {}, {}, {}

    def pass_on(p):
        cs[p].wait_recv()
        add_pair(3, p * quarter, quarter // tile)
        vs[p] = send(
            part.at[2, :, piece(p)], relay.at[:, piece(p)], rs_s.at[2 + p], rs_r.at[2 + p], dev_x if p < 2 else dev_y
        )

    for i in range(4):
        p = order[i]
        terms(3, p)
        cs[p] = send(
            tosib.at[3, :, piece(p)], fromsib.at[3, :, piece(p)], sib_s.at[3 + p], sib_r.at[3 + p], sib
        )
        if i > 0:
            pass_on(order[i - 1])
    pass_on(order[3])

    for p in order:
        vs[p].wait_recv()
        k = 1 if p < 2 else 0

        @pl.loop(0, quarter // tile)
        def _(i):
            cols = cols_at(p * quarter, i)
            part[k, :, cols] = (part[k, :, cols].astype(F32) + relay[:, cols].astype(F32)).astype(BF16)

        es[p] = send(
            part.at[k, :, piece(p)], got.at[k, :, piece(p)], rs_s.at[6 + p], rs_r.at[6 + p], dev_y if p < 2 else dev_x
        )

    def slab_sum(p, q):
        cols = cols_at(p * quarter, q)
        return own[0, :, cols] + got[0, :, cols].astype(F32) + got[1, :, cols].astype(F32)

    zc = {}
    for p in order:
        if p == order[0]:
            d_x.wait_recv()
        if p == order[1]:
            d_y.wait_recv()
        es[p].wait_recv()
        here = pl.ds(p * tile, tile)
        for r in (2, 1, 3):
            zs[r - 1, :, here] = slab_sum(p, (dp + r) % 4).astype(BF16)
            n = 3 * p + r - 1
            zc[p, r] = send(
                zs.at[r - 1, :, here], zgot.at[r - 1, :, here], z_s.at[n], z_r.at[n], zdev[r - 1]
            )
    for p in order:
        here = pl.ds(p * tile, tile)
        total = slab_sum(p, dp)
        for r in (1, 2, 3):
            zc[p, r].wait_recv()
            total = total + zgot[r - 1, :, here].astype(F32)
        out[:, here] = total.astype(BF16)

    for c in sent:
        c.wait_send()
    keep_head.wait()
    keep_gl.wait()


def rows_kernel(gl, head, out):
    out[...] = jnp.dot(gl[...], head[...], preferred_element_type=F32).astype(BF16)


def fused(hidden, head, labels, lse, cotangent, block_lists):
    tokens, width = hidden.shape
    rows = head.shape[0]
    f = lax.axis_index("fsdp")
    listed = listed_of(block_lists).astype(F32)
    order = jnp.arange(VBLOCKS, dtype=jnp.int32) ^ (f // 2)
    mine = jnp.sum(
        jnp.where(order[:, None, None] == jnp.arange(VBLOCKS)[None, None, :], listed[None, :, :], 0.0), axis=2
    )
    keep = jnp.repeat(mine, tokens // block_lists.shape[0], axis=1)
    spot = ((labels // rows) ^ f) * rows + labels % rows
    aux = jnp.concatenate(
        [lse[None], cotangent[None], spot.astype(F32)[None], jnp.zeros((1, tokens), F32), keep], axis=0
    )
    vm = pltpu.VMEM
    dma = pltpu.SemaphoreType.DMA
    any_ = pl.BlockSpec(memory_space=pl.ANY)
    vmem = pl.BlockSpec(memory_space=pltpu.VMEM)
    gl, full, owned = pl.pallas_call(
        kernel,
        out_shape=(
            jax.ShapeDtypeStruct((tokens, 8 * rows), BF16),
            jax.ShapeDtypeStruct((8, rows, width), BF16),
            jax.ShapeDtypeStruct((rows, width // 4), BF16),
        ),
        in_specs=[any_, any_, vmem],
        out_specs=(any_, any_, vmem),
        scratch_shapes=[
            vm((tokens, width), BF16), vm((8, rows, width), BF16), vm((2 * rows, tokens), F32),
            vm((tokens, 8 * rows), BF16), vm((4, 2 * rows, tokens), BF16),
            vm((4, rows, width), F32), vm((4, rows, width), BF16), vm((4, rows, width), BF16),
            vm((3, rows, width), BF16), vm((rows, width), BF16), vm((2, rows, width), BF16),
            vm((3, rows, width // 4), BF16), vm((3, rows, width // 4), BF16),
            dma((4,)), dma, dma((2,)), dma((9,)), dma((9,)), dma((7,)), dma((7,)),
            dma((10,)), dma((10,)), dma((12,)), dma((12,)),
        ],
        compiler_params=pltpu.CompilerParams(
            collective_id=0, has_side_effects=True, vmem_limit_bytes=58 * 1024 * 1024
        ),
    )(hidden, head, aux)
    wide = 1024
    grad_hidden = pl.pallas_call(
        rows_kernel,
        out_shape=jax.ShapeDtypeStruct((tokens, width), BF16),
        grid=(width // wide,),
        in_specs=[
            pl.BlockSpec((tokens, 8 * rows), lambda i: (0, 0)),
            pl.BlockSpec((8 * rows, wide), lambda i: (0, i)),
        ],
        out_specs=pl.BlockSpec((tokens, wide), lambda i: (0, i)),
        compiler_params=pltpu.CompilerParams(vmem_limit_bytes=60 * 1024 * 1024),
    )(gl, full.reshape(8 * rows, width))
    return grad_hidden, owned


def solution(mesh):
    small = mesh.shape["dp"] == 4 and mesh.shape["fsdp"] == 8
    return jax.shard_map(
        fused if small else plain,
        mesh=mesh,
        in_specs=(
            P(("dp", "fsdp"), None),
            P("fsdp", None),
            P(("dp", "fsdp")),
            P(("dp", "fsdp")),
            P(("dp", "fsdp")),
            P(("dp", "fsdp"), None),
        ),
        out_specs=(P(("dp", "fsdp"), None), P("fsdp", "dp")),
        check_vma=False,
    )
```
